32 devices in a mesh: rep: 2 (over y), node: 4 (over x, core), local: 4 (over z).
Axes of the slice: x: 2, y: 2, z: 4, core: 2. Of those that a mesh axis runs over, the one named last changes fastest.
Arguments:
- tokens: bfloat16 [8192, 4096], P(('rep', 'node', 'local')), parts along dimension 0, may hold values from -6 to 6
- routes: int32 [8192, 4], P(('rep', 'node', 'local')), parts along dimension 0, may hold values from 0 to 15, all different within a row; in each aligned block of 256 rows (0 to 255, 256 to 511, ...) at most 128 rows name the same one
- gates: int32 [8192, 4], P(('rep', 'node', 'local')), parts along dimension 0, may hold values from 4096 to 32767
- w_down: bfloat16 [4096, 1024], P('local'), may hold values from -0.09375 to 0.09375
- w_up: bfloat16 [1024, 4096], P(None, 'local'), may hold values from -0.1875 to 0.1875
- expert_gate: bfloat16 [16, 1024, 768], P(('node', 'local')), may hold values from -0.1875 to 0.1875
- expert_up: bfloat16 [16, 1024, 768], P(('node', 'local')), may hold values from -0.1875 to 0.1875
- expert_down: bfloat16 [16, 768, 1024], P(('node', 'local')), may hold values from -0.21875 to 0.21875
Outputs:
- mixed: bfloat16 [8192, 4096], P(('rep', 'node', 'local')), parts along dimension 0
The draws below stay inside these ranges and needn't reach their ends.
There are 2 independent parts, one for each index of `rep`. The reference program is written for one: setup_inputs(seed, part) draws one part's arguments, and reference() takes and returns one part's arrays. A program takes and returns all parts, laid end to end along the dimension named above; an argument that names none is the same for every part. Nothing has to cross between parts.
Inputs may be any that keep to these rules, and one draw needn't show every extreme that they name: Within the 256 rows of one device no expert is named by more than 128 routes, and in every draw some device sends exactly 128 routes to some expert; the routes of one token are distinct.
All inputs are finite; a program needn't handle non-finite values.
Results may differ from the reference program's by a relative error of at most 0.0068.
Values may be sent and summed in bfloat16 or wider, within the bound.
A program may use at most 128 MiB of HBM per device.

```python
import math
import jax
import jax.numpy as jnp
import numpy as np
from jax import lax

D = 4096
L = 1024
FF = 768
TOP = 4
TOK_DEV = 256
EXPERTS = 16
TOKENS = 4096
MOST = 128
N_NODE = 4
N_LOCAL = 4


def touch_ends(array, own_key, least, high):
    index_at = [jax.random.randint(jax.random.fold_in(own_key, axis), (), 0, length) for axis, length in enumerate(array.shape)]
    longest = array.shape.index(max(array.shape))
    next_to = index_at[:longest] + [(index_at[longest] + 1) % array.shape[longest]] + index_at[longest + 1:]
    return array.at[tuple(index_at)].set(least).at[tuple(next_to)].set(high)


def levels(stream_key, extent, cuts, low, top_value):
    def one(axis_at, shards_of):
        draws = jax.random.uniform(jax.random.fold_in(jax.random.fold_in(stream_key, 6), axis_at), (shards_of,), jnp.float32, low / len(cuts), top_value / len(cuts))
        return jnp.repeat(jnp.exp(draws), extent[axis_at] // shards_of).reshape((-1,) + (1,) * (len(extent) - axis_at - 1))

    level = one(*cuts[0])
    for cut in cuts[1:]:
        level = level * one(*cut)
    return level


def shared_out(key, own, number, rows, count, top, reach, lean):
    sequence = jax.random.permutation(key, count)
    crowded, usual = load_shares(count, rows * top, reach, lean, True), load_shares(count, rows * top, reach, lean, False)
    places = jnp.arange(count)

    def named(lengths, turn):
        used = int((lengths > 0).sum())
        fixed = max(1, used // 4)
        moved = fixed + (places - fixed + turn * (used - fixed)) % max(1, count - fixed)
        return jnp.zeros((count,), jnp.int32).at[sequence[jnp.where(places < fixed, places, moved)]].set(jnp.asarray(lengths, jnp.int32))

    lengths = jnp.where(number % 4 == 0, named(crowded, number // 4), named(usual, number - number // 4 - 1))
    mixed = jax.random.permutation(jax.random.fold_in(own, 3), count)
    source_of, sink = mixed[0:count // 2 * 2:2], mixed[1:count // 2 * 2:2]
    room = jnp.minimum(lengths[source_of] - 1, reach - lengths[sink]) // 2
    room = jnp.where((source_of == sequence[0]) | (sink == sequence[0]) | (lengths[sink] == 0), 0, jnp.maximum(room, 0))
    moved = jax.random.randint(jax.random.fold_in(own, 4), (count // 2,), 0, 1 << 20) % (room + 1)
    lengths = lengths.at[source_of].add(-moved).at[sink].add(moved)
    members = jnp.searchsorted(jnp.cumsum(lengths), jnp.arange(rows * top), side="right").astype(jnp.int32)
    table = members.reshape(top, rows).T
    table = table[jax.random.permutation(jax.random.fold_in(own, 1), rows)]
    turn = jax.random.randint(jax.random.fold_in(own, 2), (rows, 1), 0, top)
    return jnp.take_along_axis(table, (jnp.arange(top)[None, :] + turn) % top, axis=1)


def load_shares(count, total, limit, slope, full):
    portions = [(1 << 20) // math.isqrt(rank ** slope) + 1 for rank in range(1, count + 1)]
    largest = limit if full else min(limit, max(-(-total // count), total * portions[0] // sum(portions)))
    least = 1 if total - largest >= count - 1 else 0
    counts, surplus = [largest] + [least] * (count - 1), total - largest - least * (count - 1)
    while surplus > 0:
        free = [i for i in range(1, count) if counts[i] < largest] or [i for i in range(1, count) if counts[i] < limit]
        pool, left = sum([portions[i] for i in free]), surplus
        for i in free:
            extra = min(limit - counts[i], max(1, left * portions[i] // pool), surplus)
            counts[i] = counts[i] + extra
            surplus = surplus - extra
    return np.array(counts)


def normal_values(own_key, extent, scale, most, split=(), kind=jnp.bfloat16):
    drawn = jax.random.normal(own_key, extent, jnp.float32) * scale
    if len(split) > 0:
        drawn = levels(own_key, extent, split, -0.22, 0.18) * drawn
    return jnp.clip(drawn, min=-most, max=most).astype(kind)


def setup_inputs(seed: int = 0, part: int = 0) -> dict:
    streams_of = jax.random.split(jax.random.key(seed), 9)
    own_keys = jax.random.split(jax.random.fold_in(streams_of[8], part), 9)
    tokens = normal_values(own_keys[0], (TOKENS, D), 1.0, 6.0, ((0, 16),))
    routes_keys = jax.random.split(jax.random.fold_in(own_keys[1], 1), TOKENS // TOK_DEV)
    routes_turns = jax.random.permutation(jax.random.fold_in(own_keys[1], 3), TOKENS // TOK_DEV)
    routes = jax.vmap(lambda own, number: shared_out(jax.random.fold_in(own_keys[1], 2), own, number, TOK_DEV, EXPERTS, TOP, MOST, 1))(routes_keys, routes_turns).reshape((TOKENS, TOP))
    gates = touch_ends(jax.random.randint(own_keys[2], (TOKENS, TOP), 4096, 32768), jax.random.fold_in(own_keys[2], 1), 4096, 32767).astype(jnp.int32)
    w_down = normal_values(streams_of[3], (D, L), D ** -0.5, 0.09375, ((0, 4),))
    w_up = normal_values(streams_of[4], (L, D), L ** -0.5, 0.1875, ((1, 4),))
    expert_gate = normal_values(streams_of[5], (EXPERTS, L, FF), L ** -0.5, 0.1875, ((0, 16),))
    expert_up = normal_values(streams_of[6], (EXPERTS, L, FF), L ** -0.5, 0.1875, ((0, 16),))
    expert_down = normal_values(streams_of[7], (EXPERTS, FF, L), FF ** -0.5, 0.21875, ((0, 16),))
    return {"tokens": tokens, "routes": routes, "gates": gates, "w_down": w_down, "w_up": w_up, "expert_gate": expert_gate, "expert_up": expert_up, "expert_down": expert_down}


def reference(tokens, routes, gates, w_down, w_up, expert_gate, expert_up, expert_down):
    tok32 = tokens.astype(jnp.float32)
    normed = (tok32 * lax.rsqrt(lax.optimization_barrier(jnp.mean(tok32 * tok32, axis=-1, keepdims=True)) + 1e-06)).astype(jnp.bfloat16)
    latent = jnp.dot(normed, w_down, preferred_element_type=jnp.float32).astype(jnp.bfloat16)
    flat_routes = routes.reshape(-1).astype(jnp.int32)
    onehot = (flat_routes[:, None] == jnp.arange(EXPERTS, dtype=jnp.int32)[None, :]).astype(jnp.int32)
    ranks = (jnp.cumsum(onehot, axis=0) - 1).astype(jnp.int32)
    slot = lax.optimization_barrier(jnp.sum(ranks * onehot, axis=1)).astype(jnp.int32)
    per_expert = N_NODE * N_LOCAL * MOST
    target = (flat_routes * per_expert + slot).astype(jnp.int32)
    source_rows = jnp.repeat(latent, TOP, axis=0)
    buffer = jnp.zeros((EXPERTS * per_expert, L), jnp.bfloat16).at[target].set(source_rows)
    buffer = buffer.reshape(EXPERTS, per_expert, L)

    def one_expert(items):
        rows, gate_w, up_w, down_w = items
        rows32 = rows.astype(jnp.float32)
        gate = jnp.dot(rows32, gate_w.astype(jnp.float32), precision=lax.Precision.HIGHEST)
        upper = jnp.dot(rows32, up_w.astype(jnp.float32), precision=lax.Precision.HIGHEST)
        hidden = (jax.nn.silu(gate) * upper).astype(jnp.bfloat16)
        answer = jnp.dot(hidden.astype(jnp.float32), down_w.astype(jnp.float32), precision=lax.Precision.HIGHEST)
        return answer.astype(jnp.bfloat16)
    results = lax.map(one_expert, (buffer, expert_gate, expert_up, expert_down))
    results = results.reshape(EXPERTS * per_expert, L)
    picked = results[target].reshape(TOKENS, TOP, L).astype(jnp.float32)
    scale = gates.astype(jnp.float32) * (1.0 / 32768.0)
    combined = lax.optimization_barrier(jnp.sum(picked * scale[:, :, None], axis=1)).astype(jnp.bfloat16)
    lifted = jnp.dot(combined, w_up, preferred_element_type=jnp.float32)
    return (tok32 + lifted).astype(jnp.bfloat16)
```

```python
import jax
import jax.numpy as jnp
from jax import lax
from jax.sharding import PartitionSpec as P

GROUP = ("node", "local")


def gather_weight(w, axis):
    copies = lax.axis_size("rep") * lax.axis_size("node")
    part = w.shape[0] // copies
    mine = lax.axis_index("rep") * lax.axis_size("node") + lax.axis_index("node")
    piece = lax.dynamic_slice_in_dim(w, mine * part, part, axis=0)
    whole = lax.all_gather(piece, ("local", "rep", "node"), axis=0, tiled=True)
    if axis == 0:
        return whole
    n_local = lax.axis_size("local")
    return whole.reshape(n_local, w.shape[0], w.shape[1])


def local(tokens, routes, gates, w_down, w_up, expert_gate, expert_up, expert_down):
    tok_rows = tokens.shape[0]
    top_k = routes.shape[1]
    owners = lax.axis_size("node") * lax.axis_size("local")
    exp_local = expert_gate.shape[0]
    experts_all = owners * exp_local
    width = w_down.shape[1]
    capacity = 2 * tok_rows * top_k // experts_all
    me = lax.axis_index("node") * lax.axis_size("local") + lax.axis_index("local")

    coded = jnp.concatenate([routes.T, gates.T], axis=0)
    coded = lax.all_gather(coded, GROUP, axis=0)
    all_routes, all_gates = coded[:, :top_k], coded[:, top_k:]

    tok32 = tokens.astype(jnp.float32)
    normed = (tok32 * lax.rsqrt(jnp.mean(tok32 * tok32, axis=-1, keepdims=True) + 1e-06)).astype(
        jnp.bfloat16
    )
    down = gather_weight(w_down, 0)
    latent = jnp.dot(normed, down, preferred_element_type=jnp.float32).astype(jnp.bfloat16)
    everyone = lax.all_gather(latent, GROUP, axis=0)

    total = None
    for j in range(exp_local):
        named = all_routes == me * exp_local + j
        mask = jnp.any(named, axis=1)
        weight = jnp.sum(jnp.where(named, all_gates, 0), axis=1).astype(jnp.float32) * (
            1.0 / 32768.0
        )
        rank = jnp.where(mask, jnp.cumsum(mask.astype(jnp.int32), axis=1) - 1, -1)
        pick = rank[:, None, :] == jnp.arange(capacity, dtype=jnp.int32)[None, :, None]
        pick16 = pick.astype(jnp.bfloat16)
        row_weight = jnp.sum(jnp.where(pick, weight[:, None, :], 0.0), axis=2)
        rows = jnp.einsum(
            "sct,stl->scl", pick16, everyone, preferred_element_type=jnp.float32
        ).astype(jnp.bfloat16)
        rows = rows.reshape(owners * capacity, width)
        gate = jnp.dot(rows, expert_gate[j], preferred_element_type=jnp.float32)
        upper = jnp.dot(rows, expert_up[j], preferred_element_type=jnp.float32)
        hidden = (jax.nn.silu(gate) * upper).astype(jnp.bfloat16)
        answer = jnp.dot(hidden, expert_down[j], preferred_element_type=jnp.float32)
        answer = (answer * row_weight.reshape(-1, 1)).astype(jnp.bfloat16)
        placed = jnp.einsum(
            "sct,scl->stl",
            pick16,
            answer.reshape(owners, capacity, width),
            preferred_element_type=jnp.float32,
        )
        total = placed if total is None else total + placed
    total = total.astype(jnp.bfloat16).reshape(owners * tok_rows, width)
    combined = lax.psum_scatter(total, GROUP, scatter_dimension=0, tiled=True)

    up = gather_weight(w_up, 1)
    product = jnp.einsum("tl,clw->tcw", combined, up, preferred_element_type=jnp.float32)
    return (tok32 + product.reshape(tok_rows, -1)).astype(jnp.bfloat16)


def solution(mesh):
    return jax.shard_map(
        local,
        mesh=mesh,
        in_specs=(
            P(("rep", "node", "local"), None),
            P(("rep", "node", "local"), None),
            P(("rep", "node", "local"), None),
            P("local", None),
            P(None, "local"),
            P(("node", "local"), None, None),
            P(("node", "local"), None, None),
            P(("node", "local"), None, None),
        ),
        out_specs=P(("rep", "node", "local"), None),
        check_vma=False,
    )
```

```python
import jax
import jax.numpy as jnp
from jax import lax
from jax.experimental import pallas as pl
from jax.experimental.pallas import tpu as pltpu
from jax.sharding import PartitionSpec as P

GROUP = ("node", "local")


def gather_weight(w):
    part = w.shape[0] // lax.axis_size("node")
    piece = lax.dynamic_slice_in_dim(w, lax.axis_index("node") * part, part, axis=0)
    return lax.all_gather(piece, GROUP, axis=0)


def down_kernel(a_ref, w_ref, out_ref, total):
    step = pl.program_id(0)

    @pl.when(step == 0)
    def _():
        total[...] = jnp.zeros_like(total)

    total[...] += jnp.dot(a_ref[...], w_ref[0], preferred_element_type=jnp.float32)

    @pl.when(step == pl.num_programs(0) - 1)
    def _():
        out_ref[...] = total[...].astype(out_ref.dtype)


def down_project(a, pieces):
    n_node, n_local = lax.axis_size("node"), lax.axis_size("local")
    steps, part, width = pieces.shape
    ordered = a.reshape(a.shape[0], n_local, n_node, part).transpose(2, 1, 0, 3)
    ordered = ordered.reshape(steps, a.shape[0], part)
    return pl.pallas_call(
        lambda a_ref, *rest: down_kernel(a_ref.at[0], *rest),
        grid=(steps,),
        out_shape=jax.ShapeDtypeStruct((a.shape[0], width), jnp.bfloat16),
        in_specs=[
            pl.BlockSpec((1, a.shape[0], part), lambda i: (i, 0, 0)),
            pl.BlockSpec((1, part, width), lambda i: (i, 0, 0)),
        ],
        out_specs=pl.BlockSpec((a.shape[0], width), lambda i: (0, 0)),
        scratch_shapes=[pltpu.VMEM((a.shape[0], width), jnp.float32)],
        compiler_params=pltpu.CompilerParams(vmem_limit_bytes=24 * 2**20),
    )(ordered, pieces)


def up_kernel(a_ref, w_ref, tok_ref, out_ref, total):
    step = pl.program_id(1)

    @pl.when(step == 0)
    def _():
        total[...] = tok_ref[...].astype(jnp.float32)

    total[...] += jnp.dot(a_ref[...], w_ref[0], preferred_element_type=jnp.float32)

    @pl.when(step == pl.num_programs(1) - 1)
    def _():
        out_ref[...] = total[...].astype(out_ref.dtype)


def up_project(a, pieces, tokens):
    n_node, n_local = lax.axis_size("node"), lax.axis_size("local")
    _, part, columns = pieces.shape
    rows = a.shape[0]
    return pl.pallas_call(
        up_kernel,
        grid=(n_local, n_node),
        out_shape=jax.ShapeDtypeStruct(tokens.shape, jnp.bfloat16),
        in_specs=[
            pl.BlockSpec((rows, part), lambda c, k: (0, k)),
            pl.BlockSpec((1, part, columns), lambda c, k: (k * n_local + c, 0, 0)),
            pl.BlockSpec((rows, columns), lambda c, k: (0, c)),
        ],
        out_specs=pl.BlockSpec((rows, columns), lambda c, k: (0, c)),
        scratch_shapes=[pltpu.VMEM((rows, columns), jnp.float32)],
        compiler_params=pltpu.CompilerParams(vmem_limit_bytes=24 * 2**20),
    )(a, pieces, tokens)


def local(tokens, routes, gates, w_down, w_up, expert_gate, expert_up, expert_down):
    tok_rows = tokens.shape[0]
    top_k = routes.shape[1]
    owners = lax.axis_size("node") * lax.axis_size("local")
    exp_local = expert_gate.shape[0]
    experts_all = owners * exp_local
    width = w_down.shape[1]
    capacity = 2 * tok_rows * top_k // experts_all
    me = lax.axis_index("node") * lax.axis_size("local") + lax.axis_index("local")

    coded = jnp.stack([routes.T, gates.T // 256, gates.T % 256]).astype(jnp.bfloat16)
    code_rows = -(-coded.size // (16 * width)) * 16
    coded = jnp.pad(coded.reshape(-1), (0, code_rows * width - coded.size))
    coded = coded.reshape(code_rows, width)

    tok32 = tokens.astype(jnp.float32)
    normed = (tok32 * lax.rsqrt(jnp.mean(tok32 * tok32, axis=-1, keepdims=True) + 1e-06)).astype(
        jnp.bfloat16
    )
    latent = down_project(normed, gather_weight(w_down))
    everyone = lax.all_gather(jnp.concatenate([latent, coded]), GROUP, axis=0)
    codes = everyone[:, tok_rows:].reshape(owners, -1)[:, : 3 * top_k * tok_rows]
    codes = codes.astype(jnp.int32).reshape(owners, 3, top_k, tok_rows)
    all_routes = codes[:, 0]
    all_gates = codes[:, 1] * 256 + codes[:, 2]

    total = None
    for j in range(exp_local):
        named = all_routes == me * exp_local + j
        mask = jnp.any(named, axis=1)
        weight = jnp.sum(jnp.where(named, all_gates, 0), axis=1).astype(jnp.float32) * (
            1.0 / 32768.0
        )
        rank = jnp.where(mask, jnp.cumsum(mask.astype(jnp.int32), axis=1) - 1, -1)
        pick = rank[:, None, :] == jnp.arange(capacity, dtype=jnp.int32)[None, :, None]
        pick16 = pick.astype(jnp.bfloat16)
        row_weight = jnp.sum(jnp.where(pick, weight[:, None, :], 0.0), axis=2)
        longer = jnp.pad(rank, ((0, 0), (0, code_rows)), constant_values=-1)
        longer = longer[:, None, :] == jnp.arange(capacity, dtype=jnp.int32)[None, :, None]
        rows = jnp.einsum(
            "sct,stl->scl", longer.astype(jnp.bfloat16), everyone, preferred_element_type=jnp.float32
        ).astype(jnp.bfloat16)
        rows = rows.reshape(owners * capacity, width)
        gate = jnp.dot(rows, expert_gate[j], preferred_element_type=jnp.float32)
        upper = jnp.dot(rows, expert_up[j], preferred_element_type=jnp.float32)
        hidden = (jax.nn.silu(gate) * upper).astype(jnp.bfloat16)
        answer = jnp.dot(hidden, expert_down[j], preferred_element_type=jnp.float32)
        answer = (answer * row_weight.reshape(-1, 1)).astype(jnp.bfloat16)
        placed = jnp.einsum(
            "sct,scl->stl",
            pick16,
            answer.reshape(owners, capacity, width),
            preferred_element_type=jnp.float32,
        )
        total = placed if total is None else total + placed
    total = total.astype(jnp.bfloat16).reshape(owners * tok_rows, width)
    combined = lax.psum_scatter(total, GROUP, scatter_dimension=0, tiled=True)

    return up_project(combined, gather_weight(w_up), tokens)


def solution(mesh):
    return jax.shard_map(
        local,
        mesh=mesh,
        in_specs=(
            P(("rep", "node", "local"), None),
            P(("rep", "node", "local"), None),
            P(("rep", "node", "local"), None),
            P("local", None),
            P(None, "local"),
            P(("node", "local"), None, None),
            P(("node", "local"), None, None),
            P(("node", "local"), None, None),
        ),
        out_specs=P(("rep", "node", "local"), None),
        check_vma=False,
    )
```

```python
import jax
import jax.numpy as jnp
from jax import lax
from jax.experimental import pallas as pl
from jax.experimental.pallas import tpu as pltpu
from jax.sharding import PartitionSpec as P

GROUP = ("nx", "local")
PAIR = [(0, 1), (1, 0)]


def swap(x):
    return lax.ppermute(x, "core", PAIR)


def by_core(mine, theirs, axis):
    first = lax.axis_index("core") == 0
    return jnp.concatenate(
        [jnp.where(first, mine, theirs), jnp.where(first, theirs, mine)], axis=axis
    )


def gather_weight(w):
    part, half = w.shape[0] // lax.axis_size("nx"), w.shape[1] // 2
    start = (lax.axis_index("nx") * part, lax.axis_index("core") * half)
    return lax.all_gather(lax.dynamic_slice(w, start, (part, half)), GROUP, axis=0)


def down_kernel(a_ref, w_ref, out_ref, total):
    step = pl.program_id(0)

    @pl.when(step == 0)
    def _():
        total[...] = jnp.zeros_like(total)

    total[...] += jnp.dot(a_ref[...], w_ref[0], preferred_element_type=jnp.float32)

    @pl.when(step == pl.num_programs(0) - 1)
    def _():
        out_ref[...] = total[...].astype(out_ref.dtype)


def down_project(a, pieces):
    n_node, n_local = lax.axis_size("nx"), lax.axis_size("local")
    steps, part, width = pieces.shape
    ordered = a.reshape(a.shape[0], n_local, n_node, part).transpose(2, 1, 0, 3)
    ordered = ordered.reshape(steps, a.shape[0], part)
    return pl.pallas_call(
        lambda a_ref, *rest: down_kernel(a_ref.at[0], *rest),
        grid=(steps,),
        out_shape=jax.ShapeDtypeStruct((a.shape[0], width), jnp.bfloat16),
        in_specs=[
            pl.BlockSpec((1, a.shape[0], part), lambda i: (i, 0, 0)),
            pl.BlockSpec((1, part, width), lambda i: (i, 0, 0)),
        ],
        out_specs=pl.BlockSpec((a.shape[0], width), lambda i: (0, 0)),
        scratch_shapes=[pltpu.VMEM((a.shape[0], width), jnp.float32)],
        compiler_params=pltpu.CompilerParams(vmem_limit_bytes=24 * 2**20),
    )(ordered, pieces)


def up_kernel(a_ref, w_ref, tok_ref, out_ref, total):
    step = pl.program_id(1)

    @pl.when(step == 0)
    def _():
        total[...] = tok_ref[...].astype(jnp.float32)

    total[...] += jnp.dot(a_ref[...], w_ref[0], preferred_element_type=jnp.float32)

    @pl.when(step == pl.num_programs(1) - 1)
    def _():
        out_ref[...] = total[...].astype(out_ref.dtype)


def up_project(a, pieces, tokens):
    n_node, n_local = lax.axis_size("nx"), lax.axis_size("local")
    _, part, columns = pieces.shape
    rows = a.shape[0]
    return pl.pallas_call(
        up_kernel,
        grid=(n_local, n_node),
        out_shape=jax.ShapeDtypeStruct(tokens.shape, jnp.bfloat16),
        in_specs=[
            pl.BlockSpec((rows, part), lambda c, k: (0, k)),
            pl.BlockSpec((1, part, columns), lambda c, k: (k * n_local + c, 0, 0)),
            pl.BlockSpec((rows, columns), lambda c, k: (0, c)),
        ],
        out_specs=pl.BlockSpec((rows, columns), lambda c, k: (0, c)),
        scratch_shapes=[pltpu.VMEM((rows, columns), jnp.float32)],
        compiler_params=pltpu.CompilerParams(vmem_limit_bytes=24 * 2**20),
    )(a, pieces, tokens)


def local(tokens, routes, gates, w_down, w_up, expert_gate, expert_up, expert_down):
    tok_rows, model = tokens.shape
    top_k = routes.shape[1]
    n_local = lax.axis_size("local")
    chips = lax.axis_size("nx") * n_local
    exp_local = expert_gate.shape[0]
    width = w_down.shape[1]
    half = width // 2
    capacity = 2 * tok_rows * top_k // (2 * chips * exp_local)
    core = lax.axis_index("core")

    codes = jnp.concatenate([routes.T, gates.T], axis=0)
    codes = jnp.stack([codes, swap(codes)])
    coded = jnp.concatenate(
        [codes[:, :top_k], codes[:, top_k:] // 256, codes[:, top_k:] % 256], axis=1
    ).astype(jnp.bfloat16)
    code_size = coded.size
    code_rows = -(-code_size // (16 * half)) * 16
    coded = jnp.pad(coded.reshape(-1), (0, code_rows * half - code_size))
    coded = coded.reshape(code_rows, half)

    both = jnp.concatenate([tokens, swap(tokens)], axis=0)
    both32 = both.astype(jnp.float32)
    normed = (
        both32 * lax.rsqrt(jnp.mean(both32 * both32, axis=-1, keepdims=True) + 1e-06)
    ).astype(jnp.bfloat16)
    latent = down_project(normed, gather_weight(w_down))
    gathered = lax.all_gather(jnp.concatenate([latent, coded]), GROUP, axis=0)
    everyone = gathered[:, : 2 * tok_rows].reshape(chips, 2, tok_rows, half)
    codes = gathered[:, 2 * tok_rows :].reshape(chips, -1)[:, :code_size]
    codes = codes.astype(jnp.int32).reshape(chips, 2, 3, top_k, tok_rows)
    all_routes = codes[:, :, 0]
    all_gates = codes[:, :, 1] * 256 + codes[:, :, 2]

    def owner(which):
        node = lax.axis_index("nx") * 2 + which
        return (node * n_local + lax.axis_index("local")) * exp_local

    def find(expert):
        named = all_routes == expert
        mask = jnp.any(named, axis=2)
        weight = jnp.sum(jnp.where(named, all_gates, 0), axis=2)
        rank = jnp.where(mask, jnp.cumsum(mask.astype(jnp.int32), axis=2) - 1, -1)
        pick = rank[:, :, None, :] == jnp.arange(capacity, dtype=jnp.int32)[None, None, :, None]
        return pick, weight.astype(jnp.float32) * (1.0 / 32768.0)

    total = None
    for j in range(exp_local):
        pick, weight = find(owner(core) + j)
        pick_other, _ = find(owner(1 - core) + j)
        picks = jnp.concatenate([pick, pick_other], axis=2).astype(jnp.bfloat16)
        row_weight = jnp.sum(jnp.where(pick, weight[:, :, None, :], 0.0), axis=3)
        sent = jnp.einsum(
            "spct,sptl->spcl",
            pick_other.astype(jnp.bfloat16),
            everyone,
            preferred_element_type=jnp.float32,
        ).astype(jnp.bfloat16)
        theirs = swap(sent[:, ::-1])
        mine = jnp.einsum(
            "spct,sptl->spcl",
            pick.astype(jnp.bfloat16),
            everyone,
            preferred_element_type=jnp.float32,
        ).astype(jnp.bfloat16)
        rows = by_core(mine, theirs, 3).reshape(2 * chips * capacity, width)
        gate = jnp.dot(rows, expert_gate[j], preferred_element_type=jnp.float32)
        upper = jnp.dot(rows, expert_up[j], preferred_element_type=jnp.float32)
        hidden = (jax.nn.silu(gate) * upper).astype(jnp.bfloat16)
        answer = jnp.dot(hidden, expert_down[j], preferred_element_type=jnp.float32)
        answer = (answer * row_weight.reshape(-1, 1)).astype(jnp.bfloat16)
        answer = answer.reshape(chips, 2, capacity, width)
        away = lax.dynamic_slice_in_dim(answer, (1 - core) * half, half, axis=3)
        kept = lax.dynamic_slice_in_dim(answer, core * half, half, axis=3)
        answers = jnp.concatenate([kept, swap(away[:, ::-1])], axis=2)
        placed = jnp.einsum("spct,spcl->sptl", picks, answers, preferred_element_type=jnp.float32)
        total = placed if total is None else total + placed
    total = total.astype(jnp.bfloat16).reshape(chips * 2 * tok_rows, half)
    combined = lax.psum_scatter(total, GROUP, scatter_dimension=0, tiled=True)
    turned = jnp.concatenate([combined[tok_rows:], combined[:tok_rows]])
    combined = by_core(combined, swap(turned), 1)

    columns = w_up.shape[1] // 2
    residual = both.reshape(2 * tok_rows, n_local, 2, columns)
    residual = lax.dynamic_index_in_dim(residual, core, axis=2, keepdims=False)
    mixed = up_project(combined, gather_weight(w_up), residual.reshape(2 * tok_rows, -1))
    mixed = mixed.reshape(2, tok_rows, n_local, 1, columns)
    return by_core(mixed[0], swap(mixed[1]), 2).reshape(tok_rows, model)


def solution(mesh):
    shape = mesh.shape
    split = (shape["rep"], shape["node"] // 2, 2, shape["local"])
    mesh = jax.sharding.Mesh(mesh.devices.reshape(split), ("rep", "nx", "core", "local"))
    return jax.shard_map(
        local,
        mesh=mesh,
        in_specs=(
            P(("rep", "nx", "core", "local"), None),
            P(("rep", "nx", "core", "local"), None),
            P(("rep", "nx", "core", "local"), None),
            P("local", None),
            P(None, "local"),
            P(("nx", "core", "local"), None, None),
            P(("nx", "core", "local"), None, None),
            P(("nx", "core", "local"), None, None),
        ),
        out_specs=P(("rep", "nx", "core", "local"), None),
        check_vma=False,
    )
```

```python
import jax
import jax.numpy as jnp
from jax import lax
from jax.experimental import pallas as pl
from jax.experimental.pallas import tpu as pltpu
from jax.sharding import PartitionSpec as P

GROUP = ("node", "local")


def gather_weight(w):
    part = w.shape[0] // lax.axis_size("node")
    piece = lax.dynamic_slice_in_dim(w, lax.axis_index("node") * part, part, axis=0)
    return lax.all_gather(piece, GROUP, axis=0)


def gather_up(w):
    n_node, n_local = lax.axis_size("node"), lax.axis_size("local")
    here, core = lax.axis_index("local"), lax.axis_index("node") % 2
    half, columns = w.shape[0] // 2, w.shape[1]
    pair = [(i, i ^ 1) for i in range(n_node)]
    mine = lax.dynamic_slice_in_dim(w, core * half, half, axis=0)
    whole = jnp.zeros((n_local, 2, half, columns), w.dtype)
    whole = lax.dynamic_update_slice(whole, w.reshape(1, 2, half, columns), (here, 0, 0, 0))
    for way, steps in ((1, n_local // 2), (-1, (n_local - 1) // 2)):
        ring = [(i, (i + way) % n_local) for i in range(n_local)]
        block = mine
        for step in range(1, steps + 1):
            block = lax.ppermute(block, "local", ring)
            other = lax.ppermute(block, "node", pair)
            source = (here - way * step) % n_local
            whole = lax.dynamic_update_slice(whole, block[None, None], (source, core, 0, 0))
            whole = lax.dynamic_update_slice(whole, other[None, None], (source, 1 - core, 0, 0))
    return whole.reshape(n_local * 2, half, columns)


def down_kernel(a_ref, w_ref, out_ref, total):
    step = pl.program_id(0)

    @pl.when(step == 0)
    def _():
        total[...] = jnp.zeros_like(total)

    total[...] += jnp.dot(a_ref[...], w_ref[0], preferred_element_type=jnp.float32)

    @pl.when(step == pl.num_programs(0) - 1)
    def _():
        out_ref[...] = total[...].astype(out_ref.dtype)


def down_project(a, pieces):
    n_node, n_local = lax.axis_size("node"), lax.axis_size("local")
    steps, part, width = pieces.shape
    ordered = a.reshape(a.shape[0], n_local, n_node, part).transpose(2, 1, 0, 3)
    ordered = ordered.reshape(steps, a.shape[0], part)
    return pl.pallas_call(
        lambda a_ref, *rest: down_kernel(a_ref.at[0], *rest),
        grid=(steps,),
        out_shape=jax.ShapeDtypeStruct((a.shape[0], width), jnp.bfloat16),
        in_specs=[
            pl.BlockSpec((1, a.shape[0], part), lambda i: (i, 0, 0)),
            pl.BlockSpec((1, part, width), lambda i: (i, 0, 0)),
        ],
        out_specs=pl.BlockSpec((a.shape[0], width), lambda i: (0, 0)),
        scratch_shapes=[pltpu.VMEM((a.shape[0], width), jnp.float32)],
        compiler_params=pltpu.CompilerParams(vmem_limit_bytes=24 * 2**20),
    )(ordered, pieces)


def up_kernel(a_ref, w_ref, tok_ref, out_ref, total):
    step = pl.program_id(1)

    @pl.when(step == 0)
    def _():
        total[...] = tok_ref[...].astype(jnp.float32)

    total[...] += jnp.dot(a_ref[...], w_ref[0], preferred_element_type=jnp.float32)

    @pl.when(step == pl.num_programs(1) - 1)
    def _():
        out_ref[...] = total[...].astype(out_ref.dtype)


def up_project(a, pieces, tokens):
    n_local = lax.axis_size("local")
    _, part, columns = pieces.shape
    rows = a.shape[0]
    return pl.pallas_call(
        up_kernel,
        grid=(n_local, 2),
        out_shape=jax.ShapeDtypeStruct(tokens.shape, jnp.bfloat16),
        in_specs=[
            pl.BlockSpec((rows, part), lambda c, k: (0, k)),
            pl.BlockSpec((1, part, columns), lambda c, k: (c * 2 + k, 0, 0)),
            pl.BlockSpec((rows, columns), lambda c, k: (0, c)),
        ],
        out_specs=pl.BlockSpec((rows, columns), lambda c, k: (0, c)),
        scratch_shapes=[pltpu.VMEM((rows, columns), jnp.float32)],
        compiler_params=pltpu.CompilerParams(vmem_limit_bytes=24 * 2**20),
    )(a, pieces, tokens)


def local(tokens, routes, gates, w_down, w_up, expert_gate, expert_up, expert_down):
    tok_rows = tokens.shape[0]
    top_k = routes.shape[1]
    owners = lax.axis_size("node") * lax.axis_size("local")
    exp_local = expert_gate.shape[0]
    experts_all = owners * exp_local
    width = w_down.shape[1]
    capacity = 2 * tok_rows * top_k // experts_all
    me = lax.axis_index("node") * lax.axis_size("local") + lax.axis_index("local")

    coded = jnp.stack([routes.T, gates.T // 256, gates.T % 256]).astype(jnp.bfloat16)
    code_rows = -(-coded.size // (16 * width)) * 16
    coded = jnp.pad(coded.reshape(-1), (0, code_rows * width - coded.size))
    coded = coded.reshape(code_rows, width)

    tok32 = tokens.astype(jnp.float32)
    normed = (tok32 * lax.rsqrt(jnp.mean(tok32 * tok32, axis=-1, keepdims=True) + 1e-06)).astype(
        jnp.bfloat16
    )
    latent = down_project(normed, gather_weight(w_down))
    everyone = lax.all_gather(jnp.concatenate([latent, coded]), GROUP, axis=0)
    codes = everyone[:, tok_rows:].reshape(owners, -1)[:, : 3 * top_k * tok_rows]
    codes = codes.astype(jnp.int32).reshape(owners, 3, top_k, tok_rows)
    all_routes = codes[:, 0]
    all_gates = codes[:, 1] * 256 + codes[:, 2]

    total = None
    for j in range(exp_local):
        named = all_routes == me * exp_local + j
        mask = jnp.any(named, axis=1)
        weight = jnp.sum(jnp.where(named, all_gates, 0), axis=1).astype(jnp.float32) * (
            1.0 / 32768.0
        )
        rank = jnp.where(mask, jnp.cumsum(mask.astype(jnp.int32), axis=1) - 1, -1)
        pick = rank[:, None, :] == jnp.arange(capacity, dtype=jnp.int32)[None, :, None]
        pick16 = pick.astype(jnp.bfloat16)
        row_weight = jnp.sum(jnp.where(pick, weight[:, None, :], 0.0), axis=2)
        longer = jnp.pad(rank, ((0, 0), (0, code_rows)), constant_values=-1)
        longer = longer[:, None, :] == jnp.arange(capacity, dtype=jnp.int32)[None, :, None]
        rows = jnp.einsum(
            "sct,stl->scl", longer.astype(jnp.bfloat16), everyone, preferred_element_type=jnp.float32
        ).astype(jnp.bfloat16)
        rows = rows.reshape(owners * capacity, width)
        gate = jnp.dot(rows, expert_gate[j], preferred_element_type=jnp.float32)
        upper = jnp.dot(rows, expert_up[j], preferred_element_type=jnp.float32)
        hidden = (jax.nn.silu(gate) * upper).astype(jnp.bfloat16)
        answer = jnp.dot(hidden, expert_down[j], preferred_element_type=jnp.float32)
        answer = (answer * row_weight.reshape(-1, 1)).astype(jnp.bfloat16)
        placed = jnp.einsum(
            "sct,scl->stl",
            pick16,
            answer.reshape(owners, capacity, width),
            preferred_element_type=jnp.float32,
        )
        total = placed if total is None else total + placed
    total = total.astype(jnp.bfloat16).reshape(owners * tok_rows, width)
    combined = lax.psum_scatter(total, GROUP, scatter_dimension=0, tiled=True)

    return up_project(combined, gather_up(w_up), tokens)


def solution(mesh):
    return jax.shard_map(
        local,
        mesh=mesh,
        in_specs=(
            P(("rep", "node", "local"), None),
            P(("rep", "node", "local"), None),
            P(("rep", "node", "local"), None),
            P("local", None),
            P(None, "local"),
            P(("node", "local"), None, None),
            P(("node", "local"), None, None),
            P(("node", "local"), None, None),
        ),
        out_specs=P(("rep", "node", "local"), None),
        check_vma=False,
    )
```

```python
import jax
import jax.numpy as jnp
from jax import lax
from jax.experimental import pallas as pl
from jax.experimental.pallas import tpu as pltpu
from jax.sharding import PartitionSpec as P

GROUP = ("node", "local")


def gather_weight(w):
    part = w.shape[0] // lax.axis_size("node")
    piece = lax.dynamic_slice_in_dim(w, lax.axis_index("node") * part, part, axis=0)
    return lax.all_gather(piece, GROUP, axis=0)


def gather_up(w):
    n_node, n_local = lax.axis_size("node"), lax.axis_size("local")
    here, core = lax.axis_index("local"), lax.axis_index("node") % 2
    half, columns = w.shape[0] // 2, w.shape[1]
    pair = [(i, i ^ 1) for i in range(n_node)]
    mine = lax.dynamic_slice_in_dim(w, core * half, half, axis=0)
    whole = jnp.zeros((n_local, 2, half, columns), w.dtype)
    whole = lax.dynamic_update_slice(whole, w.reshape(1, 2, half, columns), (here, 0, 0, 0))
    for way, steps in ((1, n_local // 2), (-1, (n_local - 1) // 2)):
        ring = [(i, (i + way) % n_local) for i in range(n_local)]
        block = mine
        for step in range(1, steps + 1):
            block = lax.ppermute(block, "local", ring)
            other = lax.ppermute(block, "node", pair)
            source = (here - way * step) % n_local
            whole = lax.dynamic_update_slice(whole, block[None, None], (source, core, 0, 0))
            whole = lax.dynamic_update_slice(whole, other[None, None], (source, 1 - core, 0, 0))
    return whole.reshape(n_local * 2, half, columns)


def down_kernel(a_ref, w_ref, out_ref, total):
    step = pl.program_id(0)

    @pl.when(step == 0)
    def _():
        total[...] = jnp.zeros_like(total)

    total[...] += jnp.dot(a_ref[...], w_ref[0], preferred_element_type=jnp.float32)

    @pl.when(step == pl.num_programs(0) - 1)
    def _():
        out_ref[...] = total[...].astype(out_ref.dtype)


def down_project(a, pieces):
    n_node, n_local = lax.axis_size("node"), lax.axis_size("local")
    steps, part, width = pieces.shape
    ordered = a.reshape(a.shape[0], n_local, n_node, part).transpose(2, 1, 0, 3)
    ordered = ordered.reshape(steps, a.shape[0], part)
    return pl.pallas_call(
        lambda a_ref, *rest: down_kernel(a_ref.at[0], *rest),
        grid=(steps,),
        out_shape=jax.ShapeDtypeStruct((a.shape[0], width), jnp.bfloat16),
        in_specs=[
            pl.BlockSpec((1, a.shape[0], part), lambda i: (i, 0, 0)),
            pl.BlockSpec((1, part, width), lambda i: (i, 0, 0)),
        ],
        out_specs=pl.BlockSpec((a.shape[0], width), lambda i: (0, 0)),
        scratch_shapes=[pltpu.VMEM((a.shape[0], width), jnp.float32)],
        compiler_params=pltpu.CompilerParams(vmem_limit_bytes=24 * 2**20),
    )(ordered, pieces)


def up_kernel(a_ref, w_ref, tok_ref, out_ref, total):
    step = pl.program_id(1)

    @pl.when(step == 0)
    def _():
        total[...] = tok_ref[...].astype(jnp.float32)

    total[...] += jnp.dot(a_ref[...], w_ref[0], preferred_element_type=jnp.float32)

    @pl.when(step == pl.num_programs(1) - 1)
    def _():
        out_ref[...] = total[...].astype(out_ref.dtype)


def up_project(a, pieces, tokens):
    n_local = lax.axis_size("local")
    _, part, columns = pieces.shape
    rows = a.shape[0]
    return pl.pallas_call(
        up_kernel,
        grid=(n_local, 2),
        out_shape=jax.ShapeDtypeStruct(tokens.shape, jnp.bfloat16),
        in_specs=[
            pl.BlockSpec((rows, part), lambda c, k: (0, k)),
            pl.BlockSpec((1, part, columns), lambda c, k: (c * 2 + k, 0, 0)),
            pl.BlockSpec((rows, columns), lambda c, k: (0, c)),
        ],
        out_specs=pl.BlockSpec((rows, columns), lambda c, k: (0, c)),
        scratch_shapes=[pltpu.VMEM((rows, columns), jnp.float32)],
        compiler_params=pltpu.CompilerParams(vmem_limit_bytes=24 * 2**20),
    )(a, pieces, tokens)


def local(tokens, routes, gates, w_down, w_up, expert_gate, expert_up, expert_down):
    tok_rows = tokens.shape[0]
    top_k = routes.shape[1]
    owners = lax.axis_size("node") * lax.axis_size("local")
    exp_local = expert_gate.shape[0]
    experts_all = owners * exp_local
    width = w_down.shape[1]
    capacity = 2 * tok_rows * top_k // experts_all
    me = lax.axis_index("node") * lax.axis_size("local") + lax.axis_index("local")

    coded = jnp.stack([routes.T, gates.T // 256, gates.T % 256]).astype(jnp.bfloat16)
    code_rows = -(-coded.size // (16 * width)) * 16
    coded = jnp.pad(coded.reshape(-1), (0, code_rows * width - coded.size))
    coded = coded.reshape(code_rows, width)

    tok32 = tokens.astype(jnp.float32)
    normed = (tok32 * lax.rsqrt(jnp.mean(tok32 * tok32, axis=-1, keepdims=True) + 1e-06)).astype(
        jnp.bfloat16
    )
    latent = down_project(normed, gather_weight(w_down))
    up = gather_up(w_up)
    everyone = lax.all_gather(jnp.concatenate([latent, coded]), GROUP, axis=0)
    codes = everyone[:, tok_rows:].reshape(owners, -1)[:, : 3 * top_k * tok_rows]
    codes = codes.astype(jnp.int32).reshape(owners, 3, top_k, tok_rows)
    all_routes = codes[:, 0]
    all_gates = codes[:, 1] * 256 + codes[:, 2]

    total = None
    for j in range(exp_local):
        named = all_routes == me * exp_local + j
        mask = jnp.any(named, axis=1)
        weight = jnp.sum(jnp.where(named, all_gates, 0), axis=1).astype(jnp.float32) * (
            1.0 / 32768.0
        )
        rank = jnp.where(mask, jnp.cumsum(mask.astype(jnp.int32), axis=1) - 1, -1)
        pick = rank[:, None, :] == jnp.arange(capacity, dtype=jnp.int32)[None, :, None]
        pick16 = pick.astype(jnp.bfloat16)
        row_weight = jnp.sum(jnp.where(pick, weight[:, None, :], 0.0), axis=2)
        longer = jnp.pad(rank, ((0, 0), (0, code_rows)), constant_values=-1)
        longer = longer[:, None, :] == jnp.arange(capacity, dtype=jnp.int32)[None, :, None]
        rows = jnp.einsum(
            "sct,stl->scl", longer.astype(jnp.bfloat16), everyone, preferred_element_type=jnp.float32
        ).astype(jnp.bfloat16)
        rows, up = lax.optimization_barrier((rows.reshape(owners * capacity, width), up))
        gate = jnp.dot(rows, expert_gate[j], preferred_element_type=jnp.float32)
        upper = jnp.dot(rows, expert_up[j], preferred_element_type=jnp.float32)
        hidden = (jax.nn.silu(gate) * upper).astype(jnp.bfloat16)
        answer = jnp.dot(hidden, expert_down[j], preferred_element_type=jnp.float32)
        answer = (answer * row_weight.reshape(-1, 1)).astype(jnp.bfloat16)
        placed = jnp.einsum(
            "sct,scl->stl",
            pick16,
            answer.reshape(owners, capacity, width),
            preferred_element_type=jnp.float32,
        )
        total = placed if total is None else total + placed
    total = total.astype(jnp.bfloat16).reshape(owners * tok_rows, width)
    combined = lax.psum_scatter(total, GROUP, scatter_dimension=0, tiled=True)

    return up_project(combined, up, tokens)


def solution(mesh):
    return jax.shard_map(
        local,
        mesh=mesh,
        in_specs=(
            P(("rep", "node", "local"), None),
            P(("rep", "node", "local"), None),
            P(("rep", "node", "local"), None),
            P("local", None),
            P(None, "local"),
            P(("node", "local"), None, None),
            P(("node", "local"), None, None),
            P(("node", "local"), None, None),
        ),
        out_specs=P(("rep", "node", "local"), None),
        check_vma=False,
    )
```
